32 devices in a mesh: kv: 8 (over z, x), tp: 4 (over y, core).
Axes of the slice: x: 2, y: 2, z: 4, core: 2. Of those that a mesh axis runs over, the one named last changes fastest.
Arguments:
- tokens: bfloat16 [512, 8192], P(None, 'kv'), may hold values from -180 to 180
- w_query: bfloat16 [8192, 8192], P('kv', 'tp'), may hold values from -0.0625 to 0.0625
- key_matrix: bfloat16 [8192, 1024], P('kv', 'tp'), may hold values from -0.1875 to 0.1875
- value_matrix: bfloat16 [8192, 1024], P('kv', 'tp'), may hold values from -0.0625 to 0.0625
- w_out: bfloat16 [8192, 8192], P('tp', 'kv'), may hold values from -0.0625 to 0.0625
- cached_key_rows: bfloat16 [16384, 1024], P('kv', 'tp'), may hold values from -12 to 12
- cached_value_rows: bfloat16 [16384, 1024], P('kv', 'tp'), may hold values from -6 to 6
- span_count: int32 [1], replicated, may hold values from 9 to 31
Outputs:
- mixed: bfloat16 [512, 8192], P('tp', 'kv')
The draws below stay inside these ranges and needn't reach their ends.
Inputs may be any that keep to these rules, and one draw needn't show every extreme that they name: `span_count`: the new span's slot on kv device C mod 8 is free.
All inputs are finite; a program needn't handle non-finite values.
Results may differ from the reference program's by a relative error of at most 0.0095.
Values may be sent and summed in bfloat16 or wider, within the bound.
A program may use at most 128 MiB of HBM per device.

```python
import jax
import jax.numpy as jnp
from jax import lax

MODEL_WIDTH = 8192
QUERY_HEADS = 64
KEY_VALUE_HEADS = 8
HEAD_SIZE = 128
SPAN_TOKENS = 512
SLOTS = 4
CACHE_ROWS = 16384
N_KV = 8


def draw_tokens(key, part):
    key = jax.random.fold_in(key, 5)
    first_key, second_key = jax.random.split(key, 2)
    base = jnp.clip(jax.random.normal(first_key, (SPAN_TOKENS, MODEL_WIDTH), jnp.float32), -6.0, 6.0)
    boost = 30.0
    chosen = SPAN_TOKENS - 1 - jax.random.randint(second_key, (), 0, 4)
    row_scale = jnp.where(jnp.arange(SPAN_TOKENS) == chosen, boost, 1.0)
    return (base * row_scale[:, None]).astype(jnp.bfloat16)


def draw_cached_key_rows(key, part):
    key = jax.random.fold_in(key, 11)
    first_key = jax.random.fold_in(key, 0)
    value_rows = jnp.clip(jax.random.normal(first_key, (CACHE_ROWS, KEY_VALUE_HEADS * HEAD_SIZE), jnp.float32), -4.0, 4.0)
    owner = (jnp.arange(CACHE_ROWS, dtype=jnp.int32) // (SLOTS * SPAN_TOKENS)).astype(jnp.float32)
    reach = owner / max(N_KV - 1, 1)
    scales = (1.0 + 2.0 * reach)[:, None]
    value_rows = jnp.clip(value_rows * scales, -12.0, 12.0)
    return value_rows.astype(jnp.bfloat16)


def shard_levels(key, shape, cuts, low, high):
    def one(axis_at, blocks):
        steps = jax.random.uniform(jax.random.fold_in(jax.random.fold_in(key, 6), axis_at), (blocks,), jnp.float32, low / len(cuts), high / len(cuts))
        return jnp.repeat(jnp.exp(steps), shape[axis_at] // blocks).reshape((-1,) + (1,) * (len(shape) - axis_at - 1))

    loudness = one(*cuts[0])
    for cut in cuts[1:]:
        loudness = loudness * one(*cut)
    return loudness


def centred(key, shape, scale, bound, shards=(), kind=jnp.bfloat16):
    factor_of = shard_levels(key, shape, shards, -0.22, 0.18) if shards else 1.0
    values = jax.random.normal(key, shape, jnp.float32) * scale * factor_of
    return jnp.minimum(jnp.maximum(values, -bound), bound).astype(kind)


def setup_inputs(seed: int = 0) -> dict:
    seeds = jax.random.split(jax.random.key(seed), 9)
    tokens = draw_tokens(jax.random.fold_in(seeds[8], 71), 0)
    w_query = centred(seeds[1], (MODEL_WIDTH, QUERY_HEADS * HEAD_SIZE), MODEL_WIDTH ** -0.5, 0.0625, ((0, 8), (1, 4)))
    key_matrix = centred(seeds[2], (MODEL_WIDTH, KEY_VALUE_HEADS * HEAD_SIZE), (MODEL_WIDTH // 9) ** -0.5, 0.1875, ((0, 8), (1, 4)))
    value_matrix = centred(seeds[3], (MODEL_WIDTH, KEY_VALUE_HEADS * HEAD_SIZE), MODEL_WIDTH ** -0.5, 0.0625, ((0, 8), (1, 4)))
    w_out = centred(seeds[4], (QUERY_HEADS * HEAD_SIZE, MODEL_WIDTH), (QUERY_HEADS * HEAD_SIZE) ** -0.5, 0.0625, ((0, 4), (1, 8)))
    cached_key_rows = draw_cached_key_rows(jax.random.fold_in(seeds[8], 71), 0)
    cached_value_rows = centred(seeds[6], (CACHE_ROWS, KEY_VALUE_HEADS * HEAD_SIZE), 1.0, 6.0, ((0, 8), (1, 4)))
    span_count = jax.random.randint(seeds[7], (1,), N_KV + 1, N_KV * SLOTS).astype(jnp.int32)
    return {"tokens": tokens, "w_query": w_query, "key_matrix": key_matrix, "value_matrix": value_matrix, "w_out": w_out, "cached_key_rows": cached_key_rows, "cached_value_rows": cached_value_rows, "span_count": span_count}


def apply_rotary(vectors, token_positions):
    half = HEAD_SIZE // 2
    freq = 500000.0 ** (-(jnp.arange(half, dtype=jnp.float32) * 2.0) / HEAD_SIZE)
    angle = token_positions[:, None] * freq[None, :]
    cosine = jnp.cos(angle)[:, None, :]
    sine = jnp.sin(angle)[:, None, :]
    first_index = vectors[..., :half]
    second = vectors[..., half:]
    return jnp.concatenate([first_index * cosine - second * sine, second * cosine + first_index * sine], axis=-1)


def attend(state, query_rows, keys, value_rows, allowed):
    most, total, weighted = state
    scores = jnp.einsum("qgd,td->gqt", query_rows.astype(jnp.float32), keys.astype(jnp.float32)) * (HEAD_SIZE ** -0.5)
    scores = jnp.where(allowed[None], scores, -1e30)
    newest = jnp.maximum(most, jnp.max(scores, axis=-1))
    weights = jnp.where(allowed[None], jnp.exp(scores - newest[..., None]), 0.0)
    factor = jnp.exp(most - newest)
    total = total * factor + jnp.sum(weights, axis=-1)
    weighted = weighted * factor[..., None] + jnp.einsum("gqt,td->gqd", weights.astype(jnp.bfloat16).astype(jnp.float32), value_rows.astype(jnp.float32))
    return newest, total, weighted


def reference(tokens, w_query, key_matrix, value_matrix, w_out, cached_key_rows, cached_value_rows, span_count):
    spans = span_count[0]
    token_positions = (spans * SPAN_TOKENS + jnp.arange(SPAN_TOKENS, dtype=jnp.int32)).astype(jnp.float32)
    query_vector = apply_rotary(jnp.dot(tokens, w_query, preferred_element_type=jnp.float32).reshape(SPAN_TOKENS, QUERY_HEADS, HEAD_SIZE), token_positions).astype(jnp.bfloat16)
    current_key = apply_rotary(jnp.dot(tokens, key_matrix, preferred_element_type=jnp.float32).reshape(SPAN_TOKENS, KEY_VALUE_HEADS, HEAD_SIZE), token_positions).astype(jnp.bfloat16)
    current_value = jnp.dot(tokens, value_matrix, preferred_element_type=jnp.float32).reshape(SPAN_TOKENS, KEY_VALUE_HEADS, HEAD_SIZE).astype(jnp.bfloat16)
    group_queries = QUERY_HEADS // KEY_VALUE_HEADS
    query_rows = query_vector.reshape(SPAN_TOKENS, KEY_VALUE_HEADS, group_queries, HEAD_SIZE).transpose(1, 0, 2, 3)
    block_list = N_KV * SLOTS
    span_ids = (jnp.arange(N_KV, dtype=jnp.int32)[:, None] + jnp.arange(SLOTS, dtype=jnp.int32)[None, :] * N_KV).reshape(block_list)
    saved_keys = cached_key_rows.reshape(block_list, SPAN_TOKENS, KEY_VALUE_HEADS, HEAD_SIZE).transpose(2, 0, 1, 3)
    saved_values = cached_value_rows.reshape(block_list, SPAN_TOKENS, KEY_VALUE_HEADS, HEAD_SIZE).transpose(2, 0, 1, 3)
    causal = jnp.arange(SPAN_TOKENS)[:, None] >= jnp.arange(SPAN_TOKENS)[None, :]
    every = jnp.ones((SPAN_TOKENS, SPAN_TOKENS), dtype=bool)

    def per_head(items):
        head_queries, new_keys, new_values, old_keys, old_values = items
        start = (jnp.full((group_queries, SPAN_TOKENS), -1e30, jnp.float32), jnp.zeros((group_queries, SPAN_TOKENS), jnp.float32), jnp.zeros((group_queries, SPAN_TOKENS, HEAD_SIZE), jnp.float32))
        state = attend(start, head_queries, new_keys, new_values, causal)

        def step(carry, block):
            keys, value_rows, span_id = block
            allowed = jnp.logical_and(every, span_id < spans)
            return attend(carry, head_queries, keys, value_rows, allowed), None

        state, unused = lax.scan(step, state, (old_keys, old_values, span_ids))
        return state[2] / state[1][..., None]

    result = lax.map(per_head, (query_rows, current_key.transpose(1, 0, 2), current_value.transpose(1, 0, 2), saved_keys, saved_values))
    attended = result.transpose(2, 0, 1, 3).reshape(SPAN_TOKENS, QUERY_HEADS * HEAD_SIZE).astype(jnp.bfloat16)
    return jnp.dot(attended, w_out, preferred_element_type=jnp.float32).astype(jnp.bfloat16)
```

```python
import functools

import jax
import jax.numpy as jnp
from jax import lax
from jax.experimental import pallas as pl
from jax.experimental.pallas import tpu as pltpu
from jax.sharding import PartitionSpec as P

HEAD_SIZE = 128
KEY_VALUE_HEADS = 8
LOG2E = 1.4426950408889634


def apply_rotary(vectors, token_positions):
    half = HEAD_SIZE // 2
    freq = 500000.0 ** (-(jnp.arange(half, dtype=jnp.float32) * 2.0) / HEAD_SIZE)
    angle = token_positions[:, None] * freq[None, :]
    cosine = jnp.cos(angle)[:, None, :]
    sine = jnp.sin(angle)[:, None, :]
    first_index = vectors[..., :half]
    second = vectors[..., half:]
    return jnp.concatenate(
        [first_index * cosine - second * sine, second * cosine + first_index * sine], axis=-1
    )


def body(
    tokens, w_query, key_matrix, value_matrix, w_out, cached_key_rows, cached_value_rows, span_count
):
    owners = lax.axis_size("kv")
    device = lax.axis_index("kv")
    spans = span_count[0]
    q_cols = w_query.shape[1]
    k_cols = key_matrix.shape[1]
    q_heads = q_cols // HEAD_SIZE
    kv_heads = k_cols // HEAD_SIZE
    group_queries = q_heads // kv_heads
    span_rows = tokens.shape[0]
    joined = jnp.concatenate([w_query, key_matrix, value_matrix], axis=1)
    summed = lax.psum(jnp.dot(tokens, joined, preferred_element_type=jnp.float32), "kv")
    token_positions = (spans * span_rows + 0 + jnp.arange(summed.shape[0], dtype=jnp.int32)).astype(
        jnp.float32
    )
    query_part = apply_rotary(
        summed[:, :q_cols].reshape(-1, q_heads, HEAD_SIZE), token_positions
    ).reshape(-1, q_cols)
    key_part = apply_rotary(
        summed[:, q_cols : q_cols + k_cols].reshape(-1, kv_heads, HEAD_SIZE), token_positions
    ).reshape(-1, k_cols)
    projected = jnp.concatenate(
        [query_part, key_part, summed[:, q_cols + k_cols :]], axis=1
    ).astype(jnp.bfloat16)
    query_rows = projected[:, :q_cols].reshape(span_rows, kv_heads, group_queries, HEAD_SIZE)
    fresh_keys = projected[:, q_cols : q_cols + k_cols].reshape(span_rows, kv_heads, HEAD_SIZE)
    fresh_values = projected[:, q_cols + k_cols :].reshape(span_rows, kv_heads, HEAD_SIZE)
    slots = cached_key_rows.shape[0] // span_rows
    saved_keys = cached_key_rows.reshape(slots, span_rows, kv_heads, HEAD_SIZE)
    saved_values = cached_value_rows.reshape(slots, span_rows, kv_heads, HEAD_SIZE)
    causal = jnp.arange(span_rows)[:, None] >= jnp.arange(span_rows)[None, :]

    def attend(state, keys, value_rows, allowed):
        most, total, weighted = state
        scores = jnp.einsum(
            "qkgd,tkd->kgqt", query_rows, keys, preferred_element_type=jnp.float32
        ) * HEAD_SIZE ** (-0.5)
        scores = jnp.where(allowed, scores, -1e30)
        newest = jnp.maximum(most, jnp.max(scores, axis=-1))
        weights = jnp.where(allowed, jnp.exp(scores - newest[..., None]), 0.0)
        factor = jnp.exp(most - newest)
        total = total * factor + jnp.sum(weights, axis=-1)
        weighted = weighted * factor[..., None] + jnp.einsum(
            "kgqt,tkd->kgqd",
            weights.astype(jnp.bfloat16),
            value_rows,
            preferred_element_type=jnp.float32,
        )
        return (newest, total, weighted)

    def step(slot, state):
        span_id = slot * owners + device
        fresh = span_id == spans
        keys = jnp.where(fresh, fresh_keys, saved_keys[slot])
        value_rows = jnp.where(fresh, fresh_values, saved_values[slot])
        allowed = jnp.logical_or(causal, jnp.logical_not(fresh))
        return lax.cond(
            span_id <= spans,
            lambda inner: attend(inner, keys, value_rows, allowed),
            lambda inner: inner,
            state,
        )

    start = (
        jnp.full((kv_heads, group_queries, span_rows), -1e30, jnp.float32),
        jnp.zeros((kv_heads, group_queries, span_rows), jnp.float32),
        jnp.zeros((kv_heads, group_queries, span_rows, HEAD_SIZE), jnp.float32),
    )
    most, total, weighted = lax.fori_loop(0, slots, step, start)
    highest = lax.pmax(most, "kv")
    factor = jnp.exp(most - highest)
    total, weighted = (
        lax.psum((total * factor).astype(jnp.bfloat16), "kv").astype(jnp.float32),
        lax.psum((weighted * factor[..., None]).astype(jnp.bfloat16), "kv").astype(jnp.float32),
    )
    attended = (
        (weighted / total[..., None])
        .transpose(2, 0, 1, 3)
        .reshape(span_rows, q_cols)
        .astype(jnp.bfloat16)
    )
    result = lax.psum_scatter(
        jnp.dot(attended, w_out, preferred_element_type=jnp.float32),
        "tp",
        scatter_dimension=0,
        tiled=True,
    )
    return result.astype(jnp.bfloat16)


MESH_IDS = pl.DeviceIdType.MESH


def remote(source, target, send_sem, recv_sem, device):
    return pltpu.make_async_remote_copy(
        src_ref=source,
        dst_ref=target,
        send_sem=send_sem,
        recv_sem=recv_sem,
        device_id=device,
        device_id_type=MESH_IDS,
    )


def greet(peers):
    barrier = pltpu.get_barrier_semaphore()
    for peer in peers:
        pl.semaphore_signal(barrier, inc=1, device_id=peer, device_id_type=MESH_IDS)
    pl.semaphore_wait(barrier, len(peers))


def kv_position(lines, pair):
    me = lax.axis_index("kv")
    z = me // pair
    x = me % pair
    mate = {"kv": z * pair + (pair - 1 - x)}
    peers = [{"kv": ((z + 1 + i) % lines) * pair + x} for i in range(lines - 1)]
    return z, x, mate, peers


def turn(values, cosine, sine):
    parts = []
    for at in range(0, values.shape[1], HEAD_SIZE):
        u = values[:, at : at + HEAD_SIZE]
        parts.append(u * cosine + pltpu.roll(u, HEAD_SIZE // 2, 1) * sine)
    return jnp.concatenate(parts, axis=1)


def project_kernel(
    lines,
    tokens_ref,
    wq_ref,
    wk_ref,
    wv_ref,
    ck_ref,
    cv_ref,
    cos_ref,
    sin_ref,
    query_ref,
    fresh_ref,
    mate_k_ref,
    mate_v_ref,
    xsend,
    xrecv,
    own,
    zrecv,
    sent,
    xsem,
    zsem,
    gsem,
    csem,
):
    pair = 2
    chunks, rows, width = xsend.shape
    block = rows // lines
    z, x, mate, peers = kv_position(lines, pair)
    other = pair - 1 - x
    greet([mate] + peers)
    tokens = tokens_ref[...]
    half = wq_ref.shape[1] // pair

    def columns(chunk, side):
        if chunk == 0:
            at = pl.ds(pl.multiple_of(side * HEAD_SIZE, HEAD_SIZE), HEAD_SIZE)
            return jnp.concatenate([wk_ref[:, at], wv_ref[:, at]], axis=1)
        at = pl.multiple_of(side * half + (chunk - 1) * width, width)
        return wq_ref[:, pl.ds(at, width)]

    x_copies = []
    for c in range(chunks):
        xsend[c] = jnp.dot(
            tokens, columns(c, other), preferred_element_type=jnp.float32
        )
        copy = remote(xsend.at[c], xrecv.at[c], sent.at[c], xsem.at[c], mate)
        copy.start()
        x_copies.append(copy)
    for c in range(chunks):
        own[c] = jnp.dot(tokens, columns(c, x), preferred_element_type=jnp.float32)
    mine = pl.ds(pl.multiple_of(z * block, block), block)
    z_copies = []
    for c in range(chunks):
        x_copies[c].wait_recv()
        own[c] = own[c] + xrecv[c]
        group = []
        for i, peer in enumerate(peers):
            to = lax.rem(z + 1 + i, lines)
            there = pl.ds(pl.multiple_of(to * block, block), block)
            k = c * (lines - 1) + i
            copy = remote(
                own.at[c, there], zrecv.at[c, i], sent.at[chunks + k], zsem.at[k], peer
            )
            copy.start()
            group.append(copy)
        z_copies.append(group)
    there = pl.ds(pl.multiple_of(other * HEAD_SIZE, HEAD_SIZE), HEAD_SIZE)
    cache_copies = []
    base = chunks + chunks * (lines - 1)
    for i, (source, target) in enumerate(((ck_ref, mate_k_ref), (cv_ref, mate_v_ref))):
        copy = remote(source.at[:, there], target, sent.at[base + i], csem.at[i], mate)
        copy.start()
        cache_copies.append(copy)
    base += 2
    cosine, sine = cos_ref[...], sin_ref[...]
    g_copies = []
    for c in range(chunks):
        total = own[c, mine, :]
        for i in range(lines - 1):
            z_copies[c][i].wait_recv()
            total = total + zrecv[c, i]
        if c == 0:
            result = jnp.concatenate(
                [turn(total[:, :HEAD_SIZE], cosine, sine), total[:, HEAD_SIZE:]], axis=1
            )
            target = fresh_ref.at[mine]
        else:
            result = turn(total, cosine, sine)
            target = query_ref.at[c - 1, mine]
        target[...] = result.astype(jnp.bfloat16)
        for i, peer in enumerate(peers):
            k = c * (lines - 1) + i
            copy = remote(target, target, sent.at[base + k], gsem.at[k], peer)
            copy.start()
            g_copies.append(copy)
    for copy in x_copies:
        copy.wait_send()
    for group in z_copies:
        for copy in group:
            copy.wait_send()
    for copy in g_copies + cache_copies:
        copy.wait()


def project(lines, tokens, w_query, key_matrix, value_matrix, cached_k, cached_v, cosine, sine):
    rows = tokens.shape[0]
    width = 2 * HEAD_SIZE
    q_chunks = w_query.shape[1] // 2 // width
    chunks = q_chunks + 1
    cache_rows = cached_k.shape[0]
    block = rows // lines
    count = chunks * (lines - 1)
    vmem = pl.BlockSpec(memory_space=pltpu.VMEM)
    single = lambda *shape: pltpu.VMEM(shape, jnp.float32)
    return pl.pallas_call(
        functools.partial(project_kernel, lines),
        out_shape=(
            jax.ShapeDtypeStruct((q_chunks, rows, width), jnp.bfloat16),
            jax.ShapeDtypeStruct((rows, width), jnp.bfloat16),
            jax.ShapeDtypeStruct((cache_rows, HEAD_SIZE), jnp.bfloat16),
            jax.ShapeDtypeStruct((cache_rows, HEAD_SIZE), jnp.bfloat16),
        ),
        in_specs=[vmem] * 8,
        out_specs=(vmem,) * 4,
        scratch_shapes=[
            single(chunks, rows, width),
            single(chunks, rows, width),
            single(chunks, rows, width),
            single(chunks, lines - 1, block, width),
            pltpu.SemaphoreType.DMA((chunks + 2 * count + 2,)),
            pltpu.SemaphoreType.DMA((chunks,)),
            pltpu.SemaphoreType.DMA((count,)),
            pltpu.SemaphoreType.DMA((count,)),
            pltpu.SemaphoreType.DMA((2,)),
        ],
        compiler_params=pltpu.CompilerParams(
            collective_id=0, has_side_effects=True, vmem_limit_bytes=48 * 1024 * 1024
        ),
        name="project",
    )(tokens, w_query, key_matrix, value_matrix, cached_k, cached_v, cosine, sine)


def attend_kernel(
    owners,
    where_ref,
    query_ref,
    fresh_ref,
    ck_ref,
    cv_ref,
    mate_k_ref,
    mate_v_ref,
    out_ref,
    level_ref,
    most,
    weighted,
    values,
    doubled,
    scaled,
):
    me, mate, spans = where_ref[0], where_ref[1], where_ref[2]
    q_chunks, rows, width = query_ref.shape
    heads = q_chunks * 2
    slots = mate_k_ref.shape[0] // rows
    most[...] = jnp.full_like(most, -1e30)
    weighted[...] = jnp.zeros_like(weighted)
    values[:, HEAD_SIZE:] = jnp.ones((rows, HEAD_SIZE), jnp.bfloat16)

    for h in range(heads):
        at = slice((h % 2) * HEAD_SIZE, (h % 2 + 1) * HEAD_SIZE)
        exact = query_ref[h // 2, :, at].astype(jnp.float32) * (HEAD_SIZE ** (-0.5) * LOG2E)
        high = exact.astype(jnp.bfloat16)
        low = (exact - high.astype(jnp.float32)).astype(jnp.bfloat16)
        scaled[h, :, :HEAD_SIZE] = high
        scaled[h, :, HEAD_SIZE:] = low

    def visit(masked):
        def one(chunk):
            for side in range(2):
                h = chunk * 2 + side
                scores = lax.dot_general(
                    scaled[h], doubled[...], (((1,), (1,)), ((), ())), preferred_element_type=jnp.float32
                )
                if masked:
                    r = lax.broadcasted_iota(jnp.int32, scores.shape, 0)
                    t = lax.broadcasted_iota(jnp.int32, scores.shape, 1)
                    scores = jnp.where(r >= t, scores, -1e30)
                before = most[h]
                newest = jnp.maximum(before, jnp.max(scores, axis=1, keepdims=True))
                weights = jnp.exp2(scores - newest[:, :1]).astype(jnp.bfloat16)
                factor = jnp.exp2(before - newest)
                most[h] = newest
                weighted[h] = weighted[h] * jnp.concatenate(
                    [factor, factor], axis=1
                ) + jnp.dot(weights, values[...], preferred_element_type=jnp.float32)

        pl.loop(0, q_chunks)(one)

    for slot in range(slots):
        at = pl.ds(slot * rows, rows)
        for owner, k_ref, v_ref in ((me, ck_ref, cv_ref), (mate, mate_k_ref, mate_v_ref)):
            span = slot * owners + owner

            @pl.when(span < spans)
            def _():
                values[:, :HEAD_SIZE] = v_ref[at, :]
                doubled[:, :HEAD_SIZE] = k_ref[at, :]
                doubled[:, HEAD_SIZE:] = k_ref[at, :]
                visit(False)

            @pl.when(span == spans)
            def _():
                values[:, :HEAD_SIZE] = fresh_ref[:, HEAD_SIZE:]
                doubled[:, :HEAD_SIZE] = fresh_ref[:, :HEAD_SIZE]
                doubled[:, HEAD_SIZE:] = fresh_ref[:, :HEAD_SIZE]
                visit(True)

    lane = lax.broadcasted_iota(jnp.int32, (rows, HEAD_SIZE), 1)
    levels = jnp.full((rows, HEAD_SIZE), -1e30, jnp.float32)
    for h in range(heads):
        total = weighted[h, :, HEAD_SIZE:]
        seen = total > 0.0
        safe = jnp.where(seen, total, 1.0)
        out_ref[h // 2, :, (h % 2) * HEAD_SIZE : (h % 2 + 1) * HEAD_SIZE] = (
            weighted[h, :, :HEAD_SIZE] / safe
        ).astype(jnp.bfloat16)
        level = jnp.where(seen, most[h] + jnp.log(safe) * LOG2E, -1e30)
        levels = jnp.where(lane == h, level, levels)
    level_ref[...] = levels.T[: level_ref.shape[0]]


def attend(where, query, fresh, cached_k, cached_v, mate_k, mate_v, owners):
    q_chunks, rows, width = query.shape
    heads = q_chunks * 2
    cache_rows = mate_k.shape[0]
    whole = lambda *shape: pl.BlockSpec(shape, lambda i, w: (0,) * len(shape))
    mine = pl.BlockSpec((cache_rows, HEAD_SIZE), lambda i, w: (0, w[3]))
    return pl.pallas_call(
        functools.partial(attend_kernel, owners),
        grid_spec=pltpu.PrefetchScalarGridSpec(
            num_scalar_prefetch=1,
            grid=(1,),
            in_specs=[
                whole(q_chunks, rows, width),
                whole(rows, width),
                mine,
                mine,
                whole(cache_rows, HEAD_SIZE),
                whole(cache_rows, HEAD_SIZE),
            ],
            out_specs=(whole(q_chunks, rows, width), whole(heads, rows)),
            scratch_shapes=[
                pltpu.VMEM((heads, rows, HEAD_SIZE), jnp.float32),
                pltpu.VMEM((heads, rows, width), jnp.float32),
                pltpu.VMEM((rows, width), jnp.bfloat16),
                pltpu.VMEM((rows, width), jnp.bfloat16),
                pltpu.VMEM((heads, rows, width), jnp.bfloat16),
            ],
        ),
        out_shape=(
            jax.ShapeDtypeStruct((q_chunks, rows, width), jnp.bfloat16),
            jax.ShapeDtypeStruct((heads, rows), jnp.float32),
        ),
        compiler_params=pltpu.CompilerParams(vmem_limit_bytes=48 * 1024 * 1024),
        name="attend",
    )(where, query, fresh, cached_k, cached_v, mate_k, mate_v)


def combine_kernel(
    lines,
    tp,
    part_ref,
    level_ref,
    w_ref,
    out_ref,
    zrecv,
    lrecv,
    attended,
    total,
    tsend,
    trecv,
    sent,
    zsem,
    lsem,
    gsem,
    fsem,
    tsem,
):
    pair = 2
    chunks, rows, width = part_ref.shape
    heads = level_ref.shape[0]
    block = rows // lines
    z, x, mate, peers = kv_position(lines, pair)
    other = pair - 1 - x
    rank = lax.axis_index("tp")
    ranks = [{"tp": lax.rem(rank + 1 + i, tp)} for i in range(tp - 1)]
    greet([mate] + peers + ranks)
    others = lines - 1
    mine = pl.ds(pl.multiple_of(z * block, block), block)
    used = 0
    l_copies = []
    for i, peer in enumerate(peers):
        there = pl.ds(pl.multiple_of(lax.rem(z + 1 + i, lines) * block, block), block)
        copy = remote(level_ref.at[:, there], lrecv.at[i], sent.at[used], lsem.at[i], peer)
        copy.start()
        l_copies.append(copy)
        used += 1
    z_copies = []
    for c in range(chunks):
        group = []
        for i, peer in enumerate(peers):
            there = pl.ds(pl.multiple_of(lax.rem(z + 1 + i, lines) * block, block), block)
            copy = remote(
                part_ref.at[c, there],
                zrecv.at[c, i],
                sent.at[used],
                zsem.at[c * others + i],
                peer,
            )
            copy.start()
            group.append(copy)
            used += 1
        z_copies.append(group)
    for copy in l_copies:
        copy.wait_recv()
    levels = [level_ref[:, mine]] + [lrecv[i] for i in range(others)]
    top = functools.reduce(jnp.maximum, levels)
    shares = [jnp.exp2(level - top) for level in levels]
    inverse = 1.0 / functools.reduce(jnp.add, shares)
    shares = [share * inverse for share in shares]
    pad = jnp.zeros((HEAD_SIZE - heads * lines, block), jnp.float32)
    turned = jnp.concatenate(shares + [pad], axis=0).T

    g_copies = []
    f_copies = []
    for c in range(chunks):
        for copy in z_copies[c]:
            copy.wait_recv()
        sides = []
        for side in range(2):
            at = slice(side * HEAD_SIZE, (side + 1) * HEAD_SIZE)
            value = 0.0
            for i in range(lines):
                part = part_ref[c, mine, at] if i == 0 else zrecv[c, i - 1, :, at]
                lane = i * heads + c * 2 + side
                value = value + part.astype(jnp.float32) * turned[:, lane : lane + 1]
            sides.append(value)
        target = attended.at[x, c, mine]
        target[...] = jnp.concatenate(sides, axis=1).astype(jnp.bfloat16)
        group = []
        for i, peer in enumerate(peers):
            copy = remote(target, target, sent.at[used], gsem.at[c * others + i], peer)
            copy.start()
            group.append(copy)
            used += 1
        g_copies.append(group)
        copy = remote(target, target, sent.at[used], fsem.at[c * lines], mate)
        copy.start()
        f_copies.append(copy)
        used += 1
    for c in range(chunks):
        for i in range(others):
            g_copies[c][i].wait_recv()
            here = pl.ds(pl.multiple_of(lax.rem(z + others - i, lines) * block, block), block)
            target = attended.at[x, c, here]
            copy = remote(target, target, sent.at[used], fsem.at[c * lines + 1 + i], mate)
            copy.start()
            f_copies.append(copy)
            used += 1
        at = pl.multiple_of(x * chunks * width + c * width, width)
        product = jnp.dot(
            attended[x, c], w_ref[pl.ds(at, width), :], preferred_element_type=jnp.float32
        )
        total[...] = product if c == 0 else total[...] + product
    for c in range(chunks):
        f_copies[c].wait_recv()
        for i in range(others):
            f_copies[chunks + c * others + i].wait_recv()
        at = pl.multiple_of(other * chunks * width + c * width, width)
        total[...] += jnp.dot(
            attended[other, c], w_ref[pl.ds(at, width), :], preferred_element_type=jnp.float32
        )
    share = rows // tp
    t_copies = []
    for i, peer in enumerate(ranks):
        there = pl.ds(pl.multiple_of(lax.rem(rank + 1 + i, tp) * share, share), share)
        tsend[i] = total[there, :].astype(jnp.bfloat16)
        copy = remote(tsend.at[i], trecv.at[i], sent.at[used], tsem.at[i], peer)
        copy.start()
        t_copies.append(copy)
        used += 1
    result = total[pl.ds(pl.multiple_of(rank * share, share), share), :]
    for i in range(tp - 1):
        t_copies[i].wait_recv()
        result = result + trecv[i].astype(jnp.float32)
    out_ref[...] = result.astype(jnp.bfloat16)
    for copy in l_copies + f_copies + t_copies:
        copy.wait_send()
    for group in z_copies + g_copies:
        for copy in group:
            copy.wait_send()


def combine(lines, tp, part, levels, w_out):
    chunks, rows, width = part.shape
    heads = levels.shape[0]
    block = rows // lines
    share = rows // tp
    columns = w_out.shape[1]
    others = lines - 1
    sends = others + 2 * chunks * others + chunks * lines + tp - 1
    vmem = pl.BlockSpec(memory_space=pltpu.VMEM)
    dma = lambda n: pltpu.SemaphoreType.DMA((n,))
    return pl.pallas_call(
        functools.partial(combine_kernel, lines, tp),
        out_shape=jax.ShapeDtypeStruct((share, columns), jnp.bfloat16),
        in_specs=[vmem] * 3,
        out_specs=vmem,
        scratch_shapes=[
            pltpu.VMEM((chunks, others, block, width), jnp.bfloat16),
            pltpu.VMEM((others, heads, block), jnp.float32),
            pltpu.VMEM((2, chunks, rows, width), jnp.bfloat16),
            pltpu.VMEM((rows, columns), jnp.float32),
            pltpu.VMEM((tp - 1, share, columns), jnp.bfloat16),
            pltpu.VMEM((tp - 1, share, columns), jnp.bfloat16),
            dma(sends),
            dma(chunks * others),
            dma(others),
            dma(chunks * others),
            dma(chunks * lines),
            dma(tp - 1),
        ],
        compiler_params=pltpu.CompilerParams(
            collective_id=1, has_side_effects=True, vmem_limit_bytes=48 * 1024 * 1024
        ),
        name="combine",
    )(part, levels, w_out)


def fast_body(
    tokens, w_query, key_matrix, value_matrix, w_out, cached_key_rows, cached_value_rows, span_count
):
    owners = lax.axis_size("kv")
    lines = owners // 2
    me = lax.axis_index("kv")
    rows = tokens.shape[0]
    block = rows // lines
    half = HEAD_SIZE // 2
    freq = 500000.0 ** (-(jnp.arange(half, dtype=jnp.float32) * 2.0) / HEAD_SIZE)
    at = span_count[0] * rows + (me // 2) * block + jnp.arange(block, dtype=jnp.int32)
    angle = at.astype(jnp.float32)[:, None] * freq[None, :]
    cosine, sine = jnp.cos(angle), jnp.sin(angle)
    cosine = jnp.concatenate([cosine, cosine], axis=1)
    sine = jnp.concatenate([-sine, sine], axis=1)
    query, fresh, mate_k, mate_v = project(
        lines,
        tokens,
        w_query,
        key_matrix,
        value_matrix,
        cached_key_rows,
        cached_value_rows,
        cosine,
        sine,
    )
    x = me % 2
    where = jnp.stack([me, me + 1 - 2 * x, span_count[0], x]).astype(jnp.int32)
    part, levels = attend(
        where, query, fresh, cached_key_rows, cached_value_rows, mate_k, mate_v, owners
    )
    return combine(lines, lax.axis_size("tp"), part, levels, w_out)


def solution(mesh):
    paired = mesh.shape["tp"] * 2 == KEY_VALUE_HEADS and mesh.shape["kv"] == 8
    return jax.shard_map(
        fast_body if paired else body,
        mesh=mesh,
        in_specs=(
            P(None, "kv"),
            P("kv", "tp"),
            P("kv", "tp"),
            P("kv", "tp"),
            P("tp", "kv"),
            P("kv", "tp"),
            P("kv", "tp"),
            P(),
        ),
        out_specs=P("tp", "kv"),
        check_vma=False,
    )
```

```python
import functools

import jax
import jax.numpy as jnp
from jax import lax
from jax.experimental import pallas as pl
from jax.experimental.pallas import tpu as pltpu
from jax.sharding import PartitionSpec as P

HEAD_SIZE = 128
KEY_VALUE_HEADS = 8
LOG2E = 1.4426950408889634
UNROLL = 4


def apply_rotary(vectors, token_positions):
    half = HEAD_SIZE // 2
    freq = 500000.0 ** (-(jnp.arange(half, dtype=jnp.float32) * 2.0) / HEAD_SIZE)
    angle = token_positions[:, None] * freq[None, :]
    cosine = jnp.cos(angle)[:, None, :]
    sine = jnp.sin(angle)[:, None, :]
    first_index = vectors[..., :half]
    second = vectors[..., half:]
    return jnp.concatenate(
        [first_index * cosine - second * sine, second * cosine + first_index * sine], axis=-1
    )


def body(
    tokens, w_query, key_matrix, value_matrix, w_out, cached_key_rows, cached_value_rows, span_count
):
    owners = lax.axis_size("kv")
    device = lax.axis_index("kv")
    spans = span_count[0]
    q_cols = w_query.shape[1]
    k_cols = key_matrix.shape[1]
    q_heads = q_cols // HEAD_SIZE
    kv_heads = k_cols // HEAD_SIZE
    group_queries = q_heads // kv_heads
    span_rows = tokens.shape[0]
    joined = jnp.concatenate([w_query, key_matrix, value_matrix], axis=1)
    summed = lax.psum(jnp.dot(tokens, joined, preferred_element_type=jnp.float32), "kv")
    token_positions = (spans * span_rows + 0 + jnp.arange(summed.shape[0], dtype=jnp.int32)).astype(
        jnp.float32
    )
    query_part = apply_rotary(
        summed[:, :q_cols].reshape(-1, q_heads, HEAD_SIZE), token_positions
    ).reshape(-1, q_cols)
    key_part = apply_rotary(
        summed[:, q_cols : q_cols + k_cols].reshape(-1, kv_heads, HEAD_SIZE), token_positions
    ).reshape(-1, k_cols)
    projected = jnp.concatenate(
        [query_part, key_part, summed[:, q_cols + k_cols :]], axis=1
    ).astype(jnp.bfloat16)
    query_rows = projected[:, :q_cols].reshape(span_rows, kv_heads, group_queries, HEAD_SIZE)
    fresh_keys = projected[:, q_cols : q_cols + k_cols].reshape(span_rows, kv_heads, HEAD_SIZE)
    fresh_values = projected[:, q_cols + k_cols :].reshape(span_rows, kv_heads, HEAD_SIZE)
    slots = cached_key_rows.shape[0] // span_rows
    saved_keys = cached_key_rows.reshape(slots, span_rows, kv_heads, HEAD_SIZE)
    saved_values = cached_value_rows.reshape(slots, span_rows, kv_heads, HEAD_SIZE)
    causal = jnp.arange(span_rows)[:, None] >= jnp.arange(span_rows)[None, :]

    def attend(state, keys, value_rows, allowed):
        most, total, weighted = state
        scores = jnp.einsum(
            "qkgd,tkd->kgqt", query_rows, keys, preferred_element_type=jnp.float32
        ) * HEAD_SIZE ** (-0.5)
        scores = jnp.where(allowed, scores, -1e30)
        newest = jnp.maximum(most, jnp.max(scores, axis=-1))
        weights = jnp.where(allowed, jnp.exp(scores - newest[..., None]), 0.0)
        factor = jnp.exp(most - newest)
        total = total * factor + jnp.sum(weights, axis=-1)
        weighted = weighted * factor[..., None] + jnp.einsum(
            "kgqt,tkd->kgqd",
            weights.astype(jnp.bfloat16),
            value_rows,
            preferred_element_type=jnp.float32,
        )
        return (newest, total, weighted)

    def step(slot, state):
        span_id = slot * owners + device
        fresh = span_id == spans
        keys = jnp.where(fresh, fresh_keys, saved_keys[slot])
        value_rows = jnp.where(fresh, fresh_values, saved_values[slot])
        allowed = jnp.logical_or(causal, jnp.logical_not(fresh))
        return lax.cond(
            span_id <= spans,
            lambda inner: attend(inner, keys, value_rows, allowed),
            lambda inner: inner,
            state,
        )

    start = (
        jnp.full((kv_heads, group_queries, span_rows), -1e30, jnp.float32),
        jnp.zeros((kv_heads, group_queries, span_rows), jnp.float32),
        jnp.zeros((kv_heads, group_queries, span_rows, HEAD_SIZE), jnp.float32),
    )
    most, total, weighted = lax.fori_loop(0, slots, step, start)
    highest = lax.pmax(most, "kv")
    factor = jnp.exp(most - highest)
    total, weighted = (
        lax.psum((total * factor).astype(jnp.bfloat16), "kv").astype(jnp.float32),
        lax.psum((weighted * factor[..., None]).astype(jnp.bfloat16), "kv").astype(jnp.float32),
    )
    attended = (
        (weighted / total[..., None])
        .transpose(2, 0, 1, 3)
        .reshape(span_rows, q_cols)
        .astype(jnp.bfloat16)
    )
    result = lax.psum_scatter(
        jnp.dot(attended, w_out, preferred_element_type=jnp.float32),
        "tp",
        scatter_dimension=0,
        tiled=True,
    )
    return result.astype(jnp.bfloat16)


MESH_IDS = pl.DeviceIdType.MESH


def remote(source, target, send_sem, recv_sem, device):
    return pltpu.make_async_remote_copy(
        src_ref=source,
        dst_ref=target,
        send_sem=send_sem,
        recv_sem=recv_sem,
        device_id=device,
        device_id_type=MESH_IDS,
    )


def greet(peers):
    barrier = pltpu.get_barrier_semaphore()
    for peer in peers:
        pl.semaphore_signal(barrier, inc=1, device_id=peer, device_id_type=MESH_IDS)
    pl.semaphore_wait(barrier, len(peers))


def kv_position(lines, pair):
    me = lax.axis_index("kv")
    z = me // pair
    x = me % pair
    mate = {"kv": z * pair + (pair - 1 - x)}
    peers = [{"kv": ((z + 1 + i) % lines) * pair + x} for i in range(lines - 1)]
    return z, x, mate, peers


def turn(u, cosine, sine):
    return u * cosine + pltpu.roll(u, HEAD_SIZE // 2, 1) * sine


def project_kernel(
    lines,
    tokens_ref,
    wq_ref,
    wk_ref,
    wv_ref,
    ck_ref,
    cv_ref,
    cos_ref,
    sin_ref,
    query_ref,
    fresh_ref,
    mate_k_ref,
    mate_v_ref,
    xsend,
    xrecv,
    own,
    zrecv,
    sent,
    xsem,
    zsem,
    gsem,
    csem,
):
    pair = 2
    chunks, rows, width = xsend.shape
    block = rows // lines
    z, x, mate, peers = kv_position(lines, pair)
    other = pair - 1 - x
    greet([mate] + peers)
    tokens = tokens_ref[...]
    half = wq_ref.shape[1] // pair

    def columns(chunk, side):
        if chunk < 2:
            at = pl.ds(pl.multiple_of(side * HEAD_SIZE, HEAD_SIZE), HEAD_SIZE)
            return (wk_ref, wv_ref)[chunk][:, at]
        at = pl.multiple_of(side * half + (chunk - 2) * width, width)
        return wq_ref[:, pl.ds(at, width)]

    x_copies = []
    for c in range(chunks):
        xsend[c] = jnp.dot(
            tokens, columns(c, other), preferred_element_type=jnp.float32
        )
        copy = remote(xsend.at[c], xrecv.at[c], sent.at[c], xsem.at[c], mate)
        copy.start()
        x_copies.append(copy)
    for c in range(chunks):
        own[c] = jnp.dot(tokens, columns(c, x), preferred_element_type=jnp.float32)
    mine = pl.ds(pl.multiple_of(z * block, block), block)
    z_copies = []
    for c in range(chunks):
        x_copies[c].wait_recv()
        own[c] = own[c] + xrecv[c]
        group = []
        for i, peer in enumerate(peers):
            to = lax.rem(z + 1 + i, lines)
            there = pl.ds(pl.multiple_of(to * block, block), block)
            k = c * (lines - 1) + i
            copy = remote(
                own.at[c, there], zrecv.at[c, i], sent.at[chunks + k], zsem.at[k], peer
            )
            copy.start()
            group.append(copy)
        z_copies.append(group)
    there = pl.ds(pl.multiple_of(other * HEAD_SIZE, HEAD_SIZE), HEAD_SIZE)
    cache_copies = []
    base = chunks + chunks * (lines - 1)
    for i, (source, target) in enumerate(((ck_ref, mate_k_ref), (cv_ref, mate_v_ref))):
        copy = remote(source.at[:, there], target, sent.at[base + i], csem.at[i], mate)
        copy.start()
        cache_copies.append(copy)
    base += 2
    cosine, sine = cos_ref[...], sin_ref[...]
    g_copies = []
    for c in range(chunks):
        total = own[c, mine, :]
        for i in range(lines - 1):
            z_copies[c][i].wait_recv()
            total = total + zrecv[c, i]
        result = total if c == 1 else turn(total, cosine, sine)
        if c < 2:
            target = fresh_ref.at[mine, c * width : (c + 1) * width]
        else:
            target = query_ref.at[mine, (c - 2) * width : (c - 1) * width]
        target[...] = result.astype(jnp.bfloat16)
        for i, peer in enumerate(peers):
            k = c * (lines - 1) + i
            copy = remote(target, target, sent.at[base + k], gsem.at[k], peer)
            copy.start()
            g_copies.append(copy)
    for copy in x_copies:
        copy.wait_send()
    for group in z_copies:
        for copy in group:
            copy.wait_send()
    for copy in g_copies + cache_copies:
        copy.wait()


def project(lines, tokens, w_query, key_matrix, value_matrix, cached_k, cached_v, cosine, sine):
    rows = tokens.shape[0]
    width = HEAD_SIZE
    features = w_query.shape[1] // 2
    chunks = features // width + 2
    cache_rows = cached_k.shape[0]
    block = rows // lines
    count = chunks * (lines - 1)
    vmem = pl.BlockSpec(memory_space=pltpu.VMEM)
    single = lambda *shape: pltpu.VMEM(shape, jnp.float32)
    return pl.pallas_call(
        functools.partial(project_kernel, lines),
        out_shape=(
            jax.ShapeDtypeStruct((rows, features), jnp.bfloat16),
            jax.ShapeDtypeStruct((rows, 2 * width), jnp.bfloat16),
            jax.ShapeDtypeStruct((cache_rows, HEAD_SIZE), jnp.bfloat16),
            jax.ShapeDtypeStruct((cache_rows, HEAD_SIZE), jnp.bfloat16),
        ),
        in_specs=[vmem] * 8,
        out_specs=(vmem,) * 4,
        scratch_shapes=[
            single(chunks, rows, width),
            single(chunks, rows, width),
            single(chunks, rows, width),
            single(chunks, lines - 1, block, width),
            pltpu.SemaphoreType.DMA((chunks + 2 * count + 2,)),
            pltpu.SemaphoreType.DMA((chunks,)),
            pltpu.SemaphoreType.DMA((count,)),
            pltpu.SemaphoreType.DMA((count,)),
            pltpu.SemaphoreType.DMA((2,)),
        ],
        compiler_params=pltpu.CompilerParams(
            collective_id=0, has_side_effects=True, vmem_limit_bytes=48 * 1024 * 1024
        ),
        name="project",
    )(tokens, w_query, key_matrix, value_matrix, cached_k, cached_v, cosine, sine)


def attend_kernel(
    owners,
    where_ref,
    query_ref,
    fresh_ref,
    ck_ref,
    cv_ref,
    mate_k_ref,
    mate_v_ref,
    out_ref,
    level_ref,
    most,
    weighted,
    values,
    doubled,
    scaled,
):
    me, mate, spans = where_ref[0], where_ref[1], where_ref[2]
    rows, features = query_ref.shape
    heads = features // HEAD_SIZE
    slots = mate_k_ref.shape[0] // rows
    most[...] = jnp.full_like(most, -1e30)
    weighted[...] = jnp.zeros_like(weighted)
    values[:, HEAD_SIZE:] = jnp.ones((2 * rows, HEAD_SIZE), jnp.bfloat16)

    for h in range(heads):
        at = slice(h * HEAD_SIZE, (h + 1) * HEAD_SIZE)
        exact = query_ref[:, at].astype(jnp.float32) * (HEAD_SIZE ** (-0.5) * LOG2E)
        high = exact.astype(jnp.bfloat16)
        low = (exact - high.astype(jnp.float32)).astype(jnp.bfloat16)
        scaled[h, :, :HEAD_SIZE] = high
        scaled[h, :, HEAD_SIZE:] = low

    def visit(first, masked):
        def one(step):
            for side in range(UNROLL):
                h = step * UNROLL + side
                scores = lax.dot_general(
                    scaled[h], doubled[...], (((1,), (1,)), ((), ())), preferred_element_type=jnp.float32
                )
                if masked:
                    r = lax.broadcasted_iota(jnp.int32, scores.shape, 0)
                    t = lax.broadcasted_iota(jnp.int32, scores.shape, 1)
                    scores = jnp.where(t - r <= (spans - first) * rows, scores, -1e30)
                before = most[h]
                newest = jnp.maximum(before, jnp.max(scores, axis=1, keepdims=True))
                weights = jnp.exp2(scores - newest[:, :1]).astype(jnp.bfloat16)
                factor = jnp.exp2(before - newest)
                most[h] = newest
                weighted[h] = weighted[h] * jnp.concatenate(
                    [factor, factor], axis=1
                ) + jnp.dot(weights, values[...], preferred_element_type=jnp.float32)

        pl.loop(0, heads // UNROLL)(one)

    x = where_ref[3]
    for slot in range(slots):
        at = pl.ds(slot * rows, rows)
        first = slot * owners + jnp.minimum(me, mate)

        @pl.when(first <= spans)
        def _():
            for owner, to, k_ref, v_ref in (
                (me, x, ck_ref, cv_ref),
                (mate, 1 - x, mate_k_ref, mate_v_ref),
            ):
                fresh = slot * owners + owner == spans
                to = pl.ds(pl.multiple_of(to * rows, rows), rows)
                keys = jnp.where(fresh, fresh_ref[:, :HEAD_SIZE], k_ref[at, :])
                doubled[to, :HEAD_SIZE] = keys
                doubled[to, HEAD_SIZE:] = keys
                values[to, :HEAD_SIZE] = jnp.where(fresh, fresh_ref[:, HEAD_SIZE:], v_ref[at, :])

        @pl.when(first + 1 < spans)
        def _():
            visit(first, False)

        @pl.when((first == spans) | (first + 1 == spans))
        def _():
            visit(first, True)

    lane = lax.broadcasted_iota(jnp.int32, (rows, HEAD_SIZE), 1)
    levels = jnp.full((rows, HEAD_SIZE), -1e30, jnp.float32)
    for h in range(heads):
        total = weighted[h, :, HEAD_SIZE:]
        seen = total > 0.0
        safe = jnp.where(seen, total, 1.0)
        out_ref[:, h * HEAD_SIZE : (h + 1) * HEAD_SIZE] = (
            weighted[h, :, :HEAD_SIZE] / safe
        ).astype(jnp.bfloat16)
        level = jnp.where(seen, most[h] + jnp.log(safe) * LOG2E, -1e30)
        levels = jnp.where(lane == h, level, levels)
    level_ref[...] = levels.T[: level_ref.shape[0]]


def attend(where, query, fresh, cached_k, cached_v, mate_k, mate_v, owners):
    rows, features = query.shape
    heads = features // HEAD_SIZE
    width = 2 * HEAD_SIZE
    cache_rows = mate_k.shape[0]
    whole = lambda *shape: pl.BlockSpec(shape, lambda i, w: (0,) * len(shape))
    mine = pl.BlockSpec((cache_rows, HEAD_SIZE), lambda i, w: (0, w[3]))
    return pl.pallas_call(
        functools.partial(attend_kernel, owners),
        grid_spec=pltpu.PrefetchScalarGridSpec(
            num_scalar_prefetch=1,
            grid=(1,),
            in_specs=[
                whole(rows, features),
                whole(rows, width),
                mine,
                mine,
                whole(cache_rows, HEAD_SIZE),
                whole(cache_rows, HEAD_SIZE),
            ],
            out_specs=(whole(rows, features), whole(heads, rows)),
            scratch_shapes=[
                pltpu.VMEM((heads, rows, HEAD_SIZE), jnp.float32),
                pltpu.VMEM((heads, rows, width), jnp.float32),
                pltpu.VMEM((2 * rows, width), jnp.bfloat16),
                pltpu.VMEM((2 * rows, width), jnp.bfloat16),
                pltpu.VMEM((heads, rows, width), jnp.bfloat16),
            ],
        ),
        out_shape=(
            jax.ShapeDtypeStruct((rows, features), jnp.bfloat16),
            jax.ShapeDtypeStruct((heads, rows), jnp.float32),
        ),
        compiler_params=pltpu.CompilerParams(vmem_limit_bytes=48 * 1024 * 1024),
        name="attend",
    )(where, query, fresh, cached_k, cached_v, mate_k, mate_v)


def combine_kernel(
    lines,
    tp,
    part_ref,
    level_ref,
    w_ref,
    out_ref,
    zrecv,
    lrecv,
    attended,
    total,
    kept,
    tsend,
    trecv,
    sent,
    zsem,
    lsem,
    gsem,
    fsem,
    tsem,
):
    pair = 2
    rows, features = part_ref.shape
    heads = level_ref.shape[0]
    chunks = zrecv.shape[0]
    block = rows // lines
    sub = block // chunks
    z, x, mate, peers = kv_position(lines, pair)
    other = pair - 1 - x
    rank = lax.axis_index("tp")
    ranks = [{"tp": lax.rem(rank + 1 + i, tp)} for i in range(tp - 1)]
    greet([mate] + peers + ranks)
    others = lines - 1
    mine = pl.ds(pl.multiple_of(z * block, block), block)
    used = iter(range(sent.shape[0]))
    finished = []

    def start(source, target, recv_sem, device):
        copy = remote(source, target, sent.at[next(used)], recv_sem, device)
        copy.start()
        finished.append(copy)
        return copy

    l_copies = []
    for i, peer in enumerate(peers):
        there = pl.ds(pl.multiple_of(lax.rem(z + 1 + i, lines) * block, block), block)
        l_copies.append(start(level_ref.at[:, there], lrecv.at[i], lsem.at[i], peer))
    z_copies = []
    for c in range(chunks):
        for i, peer in enumerate(peers):
            at = pl.multiple_of(lax.rem(z + 1 + i, lines) * block + c * sub, sub)
            z_copies.append(
                start(
                    part_ref.at[pl.ds(at, sub)], zrecv.at[c, i], zsem.at[c * others + i], peer
                )
            )
    for copy in l_copies:
        copy.wait_recv()
    levels = [level_ref[:, mine]] + [lrecv[i] for i in range(others)]
    top = functools.reduce(jnp.maximum, levels)
    shares = [jnp.exp2(level - top) for level in levels]
    inverse = 1.0 / functools.reduce(jnp.add, shares)
    shares = [share * inverse for share in shares]
    pad = jnp.zeros((HEAD_SIZE - heads * lines, block), jnp.float32)
    turned = jnp.concatenate(shares + [pad], axis=0).T

    g_copies = {}
    f_copies = {}
    t_copies = {}

    def merge(c):
        for i in range(others):
            z_copies[c * others + i].wait_recv()
        at = pl.ds(pl.multiple_of(z * block + c * sub, sub), sub)
        merged = []
        for h in range(heads):
            cols = slice(h * HEAD_SIZE, (h + 1) * HEAD_SIZE)
            value = 0.0
            for i in range(lines):
                part = part_ref[at, cols] if i == 0 else zrecv[c, i - 1, :, cols]
                lane = i * heads + h
                factor = turned[c * sub : (c + 1) * sub, lane : lane + 1]
                value = value + part.astype(jnp.float32) * factor
            merged.append(value)
        target = attended.at[x, c, pl.ds(pl.multiple_of(z * sub, sub), sub)]
        target[...] = jnp.concatenate(merged, axis=1).astype(jnp.bfloat16)
        g_copies[c] = [
            start(target, target, gsem.at[c * others + i], peer)
            for i, peer in enumerate(peers)
        ]
        f_copies[c] = [start(target, target, fsem.at[c * lines], mate)]

    def forward(c):
        for i in range(others):
            g_copies[c][i].wait_recv()
            here = pl.ds(pl.multiple_of(lax.rem(z + others - i, lines) * sub, sub), sub)
            target = attended.at[x, c, here]
            f_copies[c].append(start(target, target, fsem.at[c * lines + 1 + i], mate))
        at = pl.ds(pl.multiple_of(x * features, features), features)
        total[c] = jnp.dot(attended[x, c], w_ref[at, :], preferred_element_type=jnp.float32)

    def finish(c):
        for copy in f_copies[c]:
            copy.wait_recv()
        at = pl.ds(pl.multiple_of(other * features, features), features)
        total[c] = total[c] + jnp.dot(
            attended[other, c], w_ref[at, :], preferred_element_type=jnp.float32
        )
        tsend[c] = total[c].astype(jnp.bfloat16)
        kept[c] = total[c, pl.ds(pl.multiple_of(rank * sub, sub), sub), :]
        t_copies[c] = []
        for i, peer in enumerate(ranks):
            there = pl.ds(pl.multiple_of(lax.rem(rank + 1 + i, tp) * sub, sub), sub)
            t_copies[c].append(
                start(tsend.at[c, there], trecv.at[c, i], tsem.at[c * (tp - 1) + i], peer)
            )

    for step in range(chunks + 2):
        if step < chunks:
            merge(step)
        if 1 <= step <= chunks:
            forward(step - 1)
        if step >= 2:
            finish(step - 2)
    for c in range(chunks):
        result = kept[c]
        for i in range(tp - 1):
            t_copies[c][i].wait_recv()
            result = result + trecv[c, i].astype(jnp.float32)
        out_ref[c * sub : (c + 1) * sub, :] = result.astype(jnp.bfloat16)
    for copy in finished:
        copy.wait_send()


def combine(lines, tp, part, levels, w_out):
    rows, features = part.shape
    heads = levels.shape[0]
    block = rows // lines
    chunks = 4
    sub = block // chunks
    columns = w_out.shape[1]
    others = lines - 1
    sends = others + chunks * (2 * others + lines + tp - 1)
    vmem = pl.BlockSpec(memory_space=pltpu.VMEM)
    dma = lambda n: pltpu.SemaphoreType.DMA((n,))
    return pl.pallas_call(
        functools.partial(combine_kernel, lines, tp),
        out_shape=jax.ShapeDtypeStruct((rows // tp, columns), jnp.bfloat16),
        in_specs=[vmem] * 3,
        out_specs=vmem,
        scratch_shapes=[
            pltpu.VMEM((chunks, others, sub, features), jnp.bfloat16),
            pltpu.VMEM((others, heads, block), jnp.float32),
            pltpu.VMEM((2, chunks, lines * sub, features), jnp.bfloat16),
            pltpu.VMEM((chunks, lines * sub, columns), jnp.float32),
            pltpu.VMEM((chunks, sub, columns), jnp.float32),
            pltpu.VMEM((chunks, lines * sub, columns), jnp.bfloat16),
            pltpu.VMEM((chunks, tp - 1, sub, columns), jnp.bfloat16),
            dma(sends),
            dma(chunks * others),
            dma(others),
            dma(chunks * others),
            dma(chunks * lines),
            dma(chunks * (tp - 1)),
        ],
        compiler_params=pltpu.CompilerParams(
            collective_id=1, has_side_effects=True, vmem_limit_bytes=48 * 1024 * 1024
        ),
        name="combine",
    )(part, levels, w_out)


def fast_body(
    tokens, w_query, key_matrix, value_matrix, w_out, cached_key_rows, cached_value_rows, span_count
):
    owners = lax.axis_size("kv")
    lines = owners // 2
    me = lax.axis_index("kv")
    rows = tokens.shape[0]
    block = rows // lines
    half = HEAD_SIZE // 2
    freq = 500000.0 ** (-(jnp.arange(half, dtype=jnp.float32) * 2.0) / HEAD_SIZE)
    at = span_count[0] * rows + (me // 2) * block + jnp.arange(block, dtype=jnp.int32)
    angle = at.astype(jnp.float32)[:, None] * freq[None, :]
    cosine, sine = jnp.cos(angle), jnp.sin(angle)
    cosine = jnp.concatenate([cosine, cosine], axis=1)
    sine = jnp.concatenate([-sine, sine], axis=1)
    query, fresh, mate_k, mate_v = project(
        lines,
        tokens,
        w_query,
        key_matrix,
        value_matrix,
        cached_key_rows,
        cached_value_rows,
        cosine,
        sine,
    )
    x = me % 2
    where = jnp.stack([me, me + 1 - 2 * x, span_count[0], x]).astype(jnp.int32)
    part, levels = attend(
        where, query, fresh, cached_key_rows, cached_value_rows, mate_k, mate_v, owners
    )
    return combine(lines, lax.axis_size("tp"), part, levels, w_out)


def solution(mesh):
    paired = mesh.shape["tp"] * 2 == KEY_VALUE_HEADS and mesh.shape["kv"] == 8
    return jax.shard_map(
        fast_body if paired else body,
        mesh=mesh,
        in_specs=(
            P(None, "kv"),
            P("kv", "tp"),
            P("kv", "tp"),
            P("kv", "tp"),
            P("tp", "kv"),
            P("kv", "tp"),
            P("kv", "tp"),
            P(),
        ),
        out_specs=P("tp", "kv"),
        check_vma=False,
    )
```

```python
import functools

import jax
import jax.numpy as jnp
from jax import lax
from jax.experimental import pallas as pl
from jax.experimental.pallas import tpu as pltpu
from jax.sharding import PartitionSpec as P

HEAD_SIZE = 128
KEY_VALUE_HEADS = 8
LOG2E = 1.4426950408889634
UNROLL = 4


def apply_rotary(vectors, token_positions):
    half = HEAD_SIZE // 2
    freq = 500000.0 ** (-(jnp.arange(half, dtype=jnp.float32) * 2.0) / HEAD_SIZE)
    angle = token_positions[:, None] * freq[None, :]
    cosine = jnp.cos(angle)[:, None, :]
    sine = jnp.sin(angle)[:, None, :]
    first_index = vectors[..., :half]
    second = vectors[..., half:]
    return jnp.concatenate(
        [first_index * cosine - second * sine, second * cosine + first_index * sine], axis=-1
    )


def body(
    tokens, w_query, key_matrix, value_matrix, w_out, cached_key_rows, cached_value_rows, span_count
):
    owners = lax.axis_size("kv")
    device = lax.axis_index("kv")
    spans = span_count[0]
    q_cols = w_query.shape[1]
    k_cols = key_matrix.shape[1]
    q_heads = q_cols // HEAD_SIZE
    kv_heads = k_cols // HEAD_SIZE
    group_queries = q_heads // kv_heads
    span_rows = tokens.shape[0]
    joined = jnp.concatenate([w_query, key_matrix, value_matrix], axis=1)
    summed = lax.psum(jnp.dot(tokens, joined, preferred_element_type=jnp.float32), "kv")
    token_positions = (spans * span_rows + 0 + jnp.arange(summed.shape[0], dtype=jnp.int32)).astype(
        jnp.float32
    )
    query_part = apply_rotary(
        summed[:, :q_cols].reshape(-1, q_heads, HEAD_SIZE), token_positions
    ).reshape(-1, q_cols)
    key_part = apply_rotary(
        summed[:, q_cols : q_cols + k_cols].reshape(-1, kv_heads, HEAD_SIZE), token_positions
    ).reshape(-1, k_cols)
    projected = jnp.concatenate(
        [query_part, key_part, summed[:, q_cols + k_cols :]], axis=1
    ).astype(jnp.bfloat16)
    query_rows = projected[:, :q_cols].reshape(span_rows, kv_heads, group_queries, HEAD_SIZE)
    fresh_keys = projected[:, q_cols : q_cols + k_cols].reshape(span_rows, kv_heads, HEAD_SIZE)
    fresh_values = projected[:, q_cols + k_cols :].reshape(span_rows, kv_heads, HEAD_SIZE)
    slots = cached_key_rows.shape[0] // span_rows
    saved_keys = cached_key_rows.reshape(slots, span_rows, kv_heads, HEAD_SIZE)
    saved_values = cached_value_rows.reshape(slots, span_rows, kv_heads, HEAD_SIZE)
    causal = jnp.arange(span_rows)[:, None] >= jnp.arange(span_rows)[None, :]

    def attend(state, keys, value_rows, allowed):
        most, total, weighted = state
        scores = jnp.einsum(
            "qkgd,tkd->kgqt", query_rows, keys, preferred_element_type=jnp.float32
        ) * HEAD_SIZE ** (-0.5)
        scores = jnp.where(allowed, scores, -1e30)
        newest = jnp.maximum(most, jnp.max(scores, axis=-1))
        weights = jnp.where(allowed, jnp.exp(scores - newest[..., None]), 0.0)
        factor = jnp.exp(most - newest)
        total = total * factor + jnp.sum(weights, axis=-1)
        weighted = weighted * factor[..., None] + jnp.einsum(
            "kgqt,tkd->kgqd",
            weights.astype(jnp.bfloat16),
            value_rows,
            preferred_element_type=jnp.float32,
        )
        return (newest, total, weighted)

    def step(slot, state):
        span_id = slot * owners + device
        fresh = span_id == spans
        keys = jnp.where(fresh, fresh_keys, saved_keys[slot])
        value_rows = jnp.where(fresh, fresh_values, saved_values[slot])
        allowed = jnp.logical_or(causal, jnp.logical_not(fresh))
        return lax.cond(
            span_id <= spans,
            lambda inner: attend(inner, keys, value_rows, allowed),
            lambda inner: inner,
            state,
        )

    start = (
        jnp.full((kv_heads, group_queries, span_rows), -1e30, jnp.float32),
        jnp.zeros((kv_heads, group_queries, span_rows), jnp.float32),
        jnp.zeros((kv_heads, group_queries, span_rows, HEAD_SIZE), jnp.float32),
    )
    most, total, weighted = lax.fori_loop(0, slots, step, start)
    highest = lax.pmax(most, "kv")
    factor = jnp.exp(most - highest)
    total, weighted = (
        lax.psum((total * factor).astype(jnp.bfloat16), "kv").astype(jnp.float32),
        lax.psum((weighted * factor[..., None]).astype(jnp.bfloat16), "kv").astype(jnp.float32),
    )
    attended = (
        (weighted / total[..., None])
        .transpose(2, 0, 1, 3)
        .reshape(span_rows, q_cols)
        .astype(jnp.bfloat16)
    )
    result = lax.psum_scatter(
        jnp.dot(attended, w_out, preferred_element_type=jnp.float32),
        "tp",
        scatter_dimension=0,
        tiled=True,
    )
    return result.astype(jnp.bfloat16)


MESH_IDS = pl.DeviceIdType.MESH


def remote(source, target, send_sem, recv_sem, device):
    return pltpu.make_async_remote_copy(
        src_ref=source,
        dst_ref=target,
        send_sem=send_sem,
        recv_sem=recv_sem,
        device_id=device,
        device_id_type=MESH_IDS,
    )


def greet(peers):
    barrier = pltpu.get_barrier_semaphore()
    for peer in peers:
        pl.semaphore_signal(barrier, inc=1, device_id=peer, device_id_type=MESH_IDS)
    pl.semaphore_wait(barrier, len(peers))


def kv_position(lines, pair):
    me = lax.axis_index("kv")
    z = me // pair
    x = me % pair
    mate = {"kv": z * pair + (pair - 1 - x)}
    peers = [{"kv": ((z + 1 + i) % lines) * pair + x} for i in range(lines - 1)]
    return z, x, mate, peers


def turn(u, cosine, sine):
    return u * cosine + pltpu.roll(u, HEAD_SIZE // 2, 1) * sine


def project_kernel(
    lines,
    tokens_ref,
    wq_ref,
    wk_ref,
    wv_ref,
    ck_ref,
    cv_ref,
    cos_ref,
    sin_ref,
    query_ref,
    fresh_ref,
    mate_k_ref,
    mate_v_ref,
    xsend,
    xrecv,
    own,
    zrecv,
    sent,
    xsem,
    zsem,
    gsem,
    csem,
):
    pair = 2
    chunks, rows, width = xsend.shape
    block = rows // lines
    z, x, mate, peers = kv_position(lines, pair)
    other = pair - 1 - x
    greet([mate] + peers)
    tokens = tokens_ref[...]
    half = wq_ref.shape[1] // pair

    def columns(chunk, side):
        if chunk < 2:
            at = pl.ds(pl.multiple_of(side * HEAD_SIZE, HEAD_SIZE), HEAD_SIZE)
            return (wk_ref, wv_ref)[chunk][:, at]
        at = pl.multiple_of(side * half + (chunk - 2) * width, width)
        return wq_ref[:, pl.ds(at, width)]

    x_copies = []
    for c in range(chunks):
        xsend[c] = jnp.dot(
            tokens, columns(c, other), preferred_element_type=jnp.float32
        )
        copy = remote(xsend.at[c], xrecv.at[c], sent.at[c], xsem.at[c], mate)
        copy.start()
        x_copies.append(copy)
    for c in range(chunks):
        own[c] = jnp.dot(tokens, columns(c, x), preferred_element_type=jnp.float32)
    near = z + 1 - 2 * (z % 2)
    far = lax.rem(z + 2, lines)
    near_device, far_device = {"kv": near * pair + x}, {"kv": far * pair + x}

    def rows_of(line):
        return pl.ds(pl.multiple_of(line * block, block), block)

    mine = rows_of(z)
    cosine, sine = cos_ref[...], sin_ref[...]
    z_copies = []
    cache_copies = []
    g_copies = []
    base = chunks + chunks * (lines - 1)

    def add_pair(c):
        x_copies[c].wait_recv()
        own[c] = own[c] + xrecv[c]
        group = []
        for i, line in enumerate((near, lax.rem(near + 2, lines))):
            k = c * (lines - 1) + i
            copy = remote(
                own.at[c, rows_of(line)],
                zrecv.at[c, i],
                sent.at[chunks + k],
                zsem.at[k],
                near_device,
            )
            copy.start()
            group.append(copy)
        z_copies.append(group)

    def add_near(c):
        for copy in z_copies[c]:
            copy.wait_recv()
        zrecv[c, 1] = zrecv[c, 1] + own[c, rows_of(far), :]
        k = c * (lines - 1) + 2
        copy = remote(
            zrecv.at[c, 1], zrecv.at[c, 2], sent.at[chunks + k], zsem.at[k], far_device
        )
        copy.start()
        z_copies[c].append(copy)

    def swap_cache():
        there = pl.ds(pl.multiple_of(other * HEAD_SIZE, HEAD_SIZE), HEAD_SIZE)
        for i, (source, target) in enumerate(((ck_ref, mate_k_ref), (cv_ref, mate_v_ref))):
            copy = remote(source.at[:, there], target, sent.at[base + i], csem.at[i], mate)
            copy.start()
            cache_copies.append(copy)

    def add_far(c):
        z_copies[c][2].wait_recv()
        total = own[c, mine, :] + zrecv[c, 0] + zrecv[c, 2]
        result = total if c == 1 else turn(total, cosine, sine)
        if c < 2:
            target = fresh_ref.at[mine, c * width : (c + 1) * width]
        else:
            target = query_ref.at[mine, (c - 2) * width : (c - 1) * width]
        target[...] = result.astype(jnp.bfloat16)
        for i, peer in enumerate(peers):
            k = c * (lines - 1) + i
            copy = remote(target, target, sent.at[base + 2 + k], gsem.at[k], peer)
            copy.start()
            g_copies.append(copy)

    for step in range(chunks + 2):
        if step < chunks:
            add_pair(step)
        if step == chunks - 1:
            swap_cache()
        if 1 <= step <= chunks:
            add_near(step - 1)
        if step >= 2:
            add_far(step - 2)
    for copy in x_copies:
        copy.wait_send()
    for group in z_copies:
        for copy in group:
            copy.wait_send()
    for copy in g_copies + cache_copies:
        copy.wait()


def project(lines, tokens, w_query, key_matrix, value_matrix, cached_k, cached_v, cosine, sine):
    rows = tokens.shape[0]
    width = HEAD_SIZE
    features = w_query.shape[1] // 2
    chunks = features // width + 2
    cache_rows = cached_k.shape[0]
    block = rows // lines
    count = chunks * (lines - 1)
    vmem = pl.BlockSpec(memory_space=pltpu.VMEM)
    single = lambda *shape: pltpu.VMEM(shape, jnp.float32)
    return pl.pallas_call(
        functools.partial(project_kernel, lines),
        out_shape=(
            jax.ShapeDtypeStruct((rows, features), jnp.bfloat16),
            jax.ShapeDtypeStruct((rows, 2 * width), jnp.bfloat16),
            jax.ShapeDtypeStruct((cache_rows, HEAD_SIZE), jnp.bfloat16),
            jax.ShapeDtypeStruct((cache_rows, HEAD_SIZE), jnp.bfloat16),
        ),
        in_specs=[vmem] * 8,
        out_specs=(vmem,) * 4,
        scratch_shapes=[
            single(chunks, rows, width),
            single(chunks, rows, width),
            single(chunks, rows, width),
            single(chunks, lines - 1, block, width),
            pltpu.SemaphoreType.DMA((chunks + 2 * count + 2,)),
            pltpu.SemaphoreType.DMA((chunks,)),
            pltpu.SemaphoreType.DMA((count,)),
            pltpu.SemaphoreType.DMA((count,)),
            pltpu.SemaphoreType.DMA((2,)),
        ],
        compiler_params=pltpu.CompilerParams(
            collective_id=0, has_side_effects=True, vmem_limit_bytes=48 * 1024 * 1024
        ),
        name="project",
    )(tokens, w_query, key_matrix, value_matrix, cached_k, cached_v, cosine, sine)


def attend_kernel(
    owners,
    where_ref,
    query_ref,
    fresh_ref,
    ck_ref,
    cv_ref,
    mate_k_ref,
    mate_v_ref,
    out_ref,
    level_ref,
    most,
    weighted,
    values,
    doubled,
    scaled,
):
    me, mate, spans = where_ref[0], where_ref[1], where_ref[2]
    rows, features = query_ref.shape
    heads = features // HEAD_SIZE
    slots = mate_k_ref.shape[0] // rows
    most[...] = jnp.full_like(most, -1e30)
    weighted[...] = jnp.zeros_like(weighted)
    values[:, HEAD_SIZE:] = jnp.ones((2 * rows, HEAD_SIZE), jnp.bfloat16)

    for h in range(heads):
        at = slice(h * HEAD_SIZE, (h + 1) * HEAD_SIZE)
        exact = query_ref[:, at].astype(jnp.float32) * (HEAD_SIZE ** (-0.5) * LOG2E)
        high = exact.astype(jnp.bfloat16)
        low = (exact - high.astype(jnp.float32)).astype(jnp.bfloat16)
        scaled[h, :, :HEAD_SIZE] = high
        scaled[h, :, HEAD_SIZE:] = low

    def visit(first, masked):
        def one(step):
            for side in range(UNROLL):
                h = step * UNROLL + side
                scores = lax.dot_general(
                    scaled[h], doubled[...], (((1,), (1,)), ((), ())), preferred_element_type=jnp.float32
                )
                if masked:
                    r = lax.broadcasted_iota(jnp.int32, scores.shape, 0)
                    t = lax.broadcasted_iota(jnp.int32, scores.shape, 1)
                    scores = jnp.where(t - r <= (spans - first) * rows, scores, -1e30)
                before = most[h]
                newest = jnp.maximum(before, jnp.max(scores, axis=1, keepdims=True))
                weights = jnp.exp2(scores - newest[:, :1]).astype(jnp.bfloat16)
                factor = jnp.exp2(before - newest)
                most[h] = newest
                weighted[h] = weighted[h] * jnp.concatenate(
                    [factor, factor], axis=1
                ) + jnp.dot(weights, values[...], preferred_element_type=jnp.float32)

        pl.loop(0, heads // UNROLL)(one)

    x = where_ref[3]
    for slot in range(slots):
        at = pl.ds(slot * rows, rows)
        first = slot * owners + jnp.minimum(me, mate)

        @pl.when(first <= spans)
        def _():
            for owner, to, k_ref, v_ref in (
                (me, x, ck_ref, cv_ref),
                (mate, 1 - x, mate_k_ref, mate_v_ref),
            ):
                fresh = slot * owners + owner == spans
                to = pl.ds(pl.multiple_of(to * rows, rows), rows)
                keys = jnp.where(fresh, fresh_ref[:, :HEAD_SIZE], k_ref[at, :])
                doubled[to, :HEAD_SIZE] = keys
                doubled[to, HEAD_SIZE:] = keys
                values[to, :HEAD_SIZE] = jnp.where(fresh, fresh_ref[:, HEAD_SIZE:], v_ref[at, :])

        @pl.when(first + 1 < spans)
        def _():
            visit(first, False)

        @pl.when((first == spans) | (first + 1 == spans))
        def _():
            visit(first, True)

    lane = lax.broadcasted_iota(jnp.int32, (rows, HEAD_SIZE), 1)
    levels = jnp.full((rows, HEAD_SIZE), -1e30, jnp.float32)
    for h in range(heads):
        total = weighted[h, :, HEAD_SIZE:]
        seen = total > 0.0
        safe = jnp.where(seen, total, 1.0)
        out_ref[:, h * HEAD_SIZE : (h + 1) * HEAD_SIZE] = (
            weighted[h, :, :HEAD_SIZE] / safe
        ).astype(jnp.bfloat16)
        level = jnp.where(seen, most[h] + jnp.log(safe) * LOG2E, -1e30)
        levels = jnp.where(lane == h, level, levels)
    level_ref[...] = levels.T[: level_ref.shape[0]]


def attend(where, query, fresh, cached_k, cached_v, mate_k, mate_v, owners):
    rows, features = query.shape
    heads = features // HEAD_SIZE
    width = 2 * HEAD_SIZE
    cache_rows = mate_k.shape[0]
    whole = lambda *shape: pl.BlockSpec(shape, lambda i, w: (0,) * len(shape))
    mine = pl.BlockSpec((cache_rows, HEAD_SIZE), lambda i, w: (0, w[3]))
    return pl.pallas_call(
        functools.partial(attend_kernel, owners),
        grid_spec=pltpu.PrefetchScalarGridSpec(
            num_scalar_prefetch=1,
            grid=(1,),
            in_specs=[
                whole(rows, features),
                whole(rows, width),
                mine,
                mine,
                whole(cache_rows, HEAD_SIZE),
                whole(cache_rows, HEAD_SIZE),
            ],
            out_specs=(whole(rows, features), whole(heads, rows)),
            scratch_shapes=[
                pltpu.VMEM((heads, rows, HEAD_SIZE), jnp.float32),
                pltpu.VMEM((heads, rows, width), jnp.float32),
                pltpu.VMEM((2 * rows, width), jnp.bfloat16),
                pltpu.VMEM((2 * rows, width), jnp.bfloat16),
                pltpu.VMEM((heads, rows, width), jnp.bfloat16),
            ],
        ),
        out_shape=(
            jax.ShapeDtypeStruct((rows, features), jnp.bfloat16),
            jax.ShapeDtypeStruct((heads, rows), jnp.float32),
        ),
        compiler_params=pltpu.CompilerParams(vmem_limit_bytes=48 * 1024 * 1024),
        name="attend",
    )(where, query, fresh, cached_k, cached_v, mate_k, mate_v)


def combine_kernel(
    lines,
    tp,
    part_ref,
    level_ref,
    w_ref,
    out_ref,
    zrecv,
    lrecv,
    attended,
    total,
    kept,
    tsend,
    trecv,
    sent,
    zsem,
    lsem,
    gsem,
    fsem,
    tsem,
):
    pair = 2
    rows, features = part_ref.shape
    heads = level_ref.shape[0]
    chunks = zrecv.shape[0]
    block = rows // lines
    sub = block // chunks
    z, x, mate, peers = kv_position(lines, pair)
    other = pair - 1 - x
    rank = lax.axis_index("tp")
    ranks = [{"tp": lax.rem(rank + 1 + i, tp)} for i in range(tp - 1)]
    greet([mate] + peers + ranks)
    others = lines - 1
    mine = pl.ds(pl.multiple_of(z * block, block), block)
    used = iter(range(sent.shape[0]))
    finished = []

    def start(source, target, recv_sem, device):
        copy = remote(source, target, sent.at[next(used)], recv_sem, device)
        copy.start()
        finished.append(copy)
        return copy

    l_copies = []
    for i, peer in enumerate(peers):
        there = pl.ds(pl.multiple_of(lax.rem(z + 1 + i, lines) * block, block), block)
        l_copies.append(start(level_ref.at[:, there], lrecv.at[i], lsem.at[i], peer))
    z_copies = []
    for c in range(chunks):
        for i, peer in enumerate(peers):
            at = pl.multiple_of(lax.rem(z + 1 + i, lines) * block + c * sub, sub)
            z_copies.append(
                start(
                    part_ref.at[pl.ds(at, sub)], zrecv.at[c, i], zsem.at[c * others + i], peer
                )
            )
    for copy in l_copies:
        copy.wait_recv()
    levels = [level_ref[:, mine]] + [lrecv[i] for i in range(others)]
    top = functools.reduce(jnp.maximum, levels)
    shares = [jnp.exp2(level - top) for level in levels]
    inverse = 1.0 / functools.reduce(jnp.add, shares)
    shares = [share * inverse for share in shares]
    pad = jnp.zeros((HEAD_SIZE - heads * lines, block), jnp.float32)
    turned = jnp.concatenate(shares + [pad], axis=0).T

    g_copies = {}
    f_copies = {}
    t_copies = {}

    def merge(c):
        for i in range(others):
            z_copies[c * others + i].wait_recv()
        at = pl.ds(pl.multiple_of(z * block + c * sub, sub), sub)
        merged = []
        for h in range(heads):
            cols = slice(h * HEAD_SIZE, (h + 1) * HEAD_SIZE)
            value = 0.0
            for i in range(lines):
                part = part_ref[at, cols] if i == 0 else zrecv[c, i - 1, :, cols]
                lane = i * heads + h
                factor = turned[c * sub : (c + 1) * sub, lane : lane + 1]
                value = value + part.astype(jnp.float32) * factor
            merged.append(value)
        target = attended.at[x, c, pl.ds(pl.multiple_of(z * sub, sub), sub)]
        target[...] = jnp.concatenate(merged, axis=1).astype(jnp.bfloat16)
        g_copies[c] = [
            start(target, target, gsem.at[c * others + i], peer)
            for i, peer in enumerate(peers)
        ]
        f_copies[c] = [start(target, target, fsem.at[c * lines], mate)]

    def forward(c):
        for i in range(others):
            g_copies[c][i].wait_recv()
            here = pl.ds(pl.multiple_of(lax.rem(z + others - i, lines) * sub, sub), sub)
            target = attended.at[x, c, here]
            f_copies[c].append(start(target, target, fsem.at[c * lines + 1 + i], mate))
        at = pl.ds(pl.multiple_of(x * features, features), features)
        total[c] = jnp.dot(attended[x, c], w_ref[at, :], preferred_element_type=jnp.float32)

    def finish(c):
        for copy in f_copies[c]:
            copy.wait_recv()
        at = pl.ds(pl.multiple_of(other * features, features), features)
        total[c] = total[c] + jnp.dot(
            attended[other, c], w_ref[at, :], preferred_element_type=jnp.float32
        )
        tsend[c] = total[c].astype(jnp.bfloat16)
        kept[c] = total[c, pl.ds(pl.multiple_of(rank * sub, sub), sub), :]
        t_copies[c] = []
        for i, peer in enumerate(ranks):
            there = pl.ds(pl.multiple_of(lax.rem(rank + 1 + i, tp) * sub, sub), sub)
            t_copies[c].append(
                start(tsend.at[c, there], trecv.at[c, i], tsem.at[c * (tp - 1) + i], peer)
            )

    for step in range(chunks + 2):
        if step < chunks:
            merge(step)
        if 1 <= step <= chunks:
            forward(step - 1)
        if step >= 2:
            finish(step - 2)
    for c in range(chunks):
        result = kept[c]
        for i in range(tp - 1):
            t_copies[c][i].wait_recv()
            result = result + trecv[c, i].astype(jnp.float32)
        out_ref[c * sub : (c + 1) * sub, :] = result.astype(jnp.bfloat16)
    for copy in finished:
        copy.wait_send()


def combine(lines, tp, part, levels, w_out):
    rows, features = part.shape
    heads = levels.shape[0]
    block = rows // lines
    chunks = 4
    sub = block // chunks
    columns = w_out.shape[1]
    others = lines - 1
    sends = others + chunks * (2 * others + lines + tp - 1)
    vmem = pl.BlockSpec(memory_space=pltpu.VMEM)
    dma = lambda n: pltpu.SemaphoreType.DMA((n,))
    return pl.pallas_call(
        functools.partial(combine_kernel, lines, tp),
        out_shape=jax.ShapeDtypeStruct((rows // tp, columns), jnp.bfloat16),
        in_specs=[vmem] * 3,
        out_specs=vmem,
        scratch_shapes=[
            pltpu.VMEM((chunks, others, sub, features), jnp.bfloat16),
            pltpu.VMEM((others, heads, block), jnp.float32),
            pltpu.VMEM((2, chunks, lines * sub, features), jnp.bfloat16),
            pltpu.VMEM((chunks, lines * sub, columns), jnp.float32),
            pltpu.VMEM((chunks, sub, columns), jnp.float32),
            pltpu.VMEM((chunks, lines * sub, columns), jnp.bfloat16),
            pltpu.VMEM((chunks, tp - 1, sub, columns), jnp.bfloat16),
            dma(sends),
            dma(chunks * others),
            dma(others),
            dma(chunks * others),
            dma(chunks * lines),
            dma(chunks * (tp - 1)),
        ],
        compiler_params=pltpu.CompilerParams(
            collective_id=1, has_side_effects=True, vmem_limit_bytes=48 * 1024 * 1024
        ),
        name="combine",
    )(part, levels, w_out)


def fast_body(
    tokens, w_query, key_matrix, value_matrix, w_out, cached_key_rows, cached_value_rows, span_count
):
    owners = lax.axis_size("kv")
    lines = owners // 2
    me = lax.axis_index("kv")
    rows = tokens.shape[0]
    block = rows // lines
    half = HEAD_SIZE // 2
    freq = 500000.0 ** (-(jnp.arange(half, dtype=jnp.float32) * 2.0) / HEAD_SIZE)
    at = span_count[0] * rows + (me // 2) * block + jnp.arange(block, dtype=jnp.int32)
    angle = at.astype(jnp.float32)[:, None] * freq[None, :]
    cosine, sine = jnp.cos(angle), jnp.sin(angle)
    cosine = jnp.concatenate([cosine, cosine], axis=1)
    sine = jnp.concatenate([-sine, sine], axis=1)
    query, fresh, mate_k, mate_v = project(
        lines,
        tokens,
        w_query,
        key_matrix,
        value_matrix,
        cached_key_rows,
        cached_value_rows,
        cosine,
        sine,
    )
    x = me % 2
    where = jnp.stack([me, me + 1 - 2 * x, span_count[0], x]).astype(jnp.int32)
    part, levels = attend(
        where, query, fresh, cached_key_rows, cached_value_rows, mate_k, mate_v, owners
    )
    return combine(lines, lax.axis_size("tp"), part, levels, w_out)


def solution(mesh):
    paired = mesh.shape["tp"] * 2 == KEY_VALUE_HEADS and mesh.shape["kv"] == 2 * 4
    return jax.shard_map(
        fast_body if paired else body,
        mesh=mesh,
        in_specs=(
            P(None, "kv"),
            P("kv", "tp"),
            P("kv", "tp"),
            P("kv", "tp"),
            P("tp", "kv"),
            P("kv", "tp"),
            P("kv", "tp"),
            P(),
        ),
        out_specs=P("tp", "kv"),
        check_vma=False,
    )
```
